32 devices in a mesh: pair: 2 (over x), blk: 4 (over z), rows: 4 (over y, core).
Axes of the slice: x: 2, y: 2, z: 4, core: 2. Of those that a mesh axis runs over, the one named last changes fastest.
Arguments:
- tiles: float32 [2, 2048, 131072], P('pair', None, ('blk', 'rows')), may hold values from -0.0234375 to 0.0234375
- trial: float32 [2, 131072, 1024], P('pair', ('blk', 'rows')), may hold values from -6 to 6
Outputs:
- products: float32 [2, 2048, 1024], P('pair', ('blk', 'rows'))
The draws below stay inside these ranges and needn't reach their ends.
All inputs are finite; a program needn't handle non-finite values.
Results may differ from the reference program's by a relative error of at most 0.000076.
Values sent between devices are 32-bit elements; how exact they have to be, the bound alone decides.
No kernel may reach another device: no remote copies, remote signals or barrier semaphores. Data moves between devices by JAX's collectives and lax.ppermute only.
A program may use at most 256 MiB of HBM per device.

```python
import jax
import jax.numpy as jnp
from jax import lax

N = 131072
W = 2048
K = 1024


def spiked(drawn, own_key, source, target, blocks, factor):
    owner, partner = [(jnp.arange(drawn.shape[dim]) // (drawn.shape[dim] // blocks)).reshape([-1 if axis == dim else 1 for axis in range(drawn.ndim)]) for dim in (source, target)]
    chosen = jax.random.permutation(own_key, blocks)[partner]
    strong = (owner == chosen) | (owner == (partner + blocks // 2) % blocks)
    return jnp.where(strong, factor * drawn, drawn)


def block_scale(key, extent, pieces, low, high):
    loudness, own = 1.0, jax.random.fold_in(key, 6)
    for position, shards_of in pieces:
        heights = jnp.exp(jax.random.uniform(jax.random.fold_in(own, position), (shards_of,), jnp.float32, low / len(pieces), high / len(pieces)))
        loudness = loudness * jnp.repeat(heights, extent[position] // shards_of).reshape([-1 if axis == position else 1 for axis in range(len(extent))])
    return loudness


def centred(key, shape, spread, bound, pieces=(), held_as=jnp.bfloat16):
    result = spread * jax.random.normal(key, shape, jnp.float32)
    if pieces:
        result = result * block_scale(key, shape, pieces, -0.22, 0.18)
    return jnp.clip(result, -bound, bound).astype(held_as)


def noise_with(rng, dims, scale, limit, split, heavy, kind=jnp.bfloat16):
    result = scale * jax.random.normal(rng, dims, jnp.float32)
    if split:
        result = result * block_scale(rng, dims, split, -0.22, 0.18)
    return jnp.clip(spiked(result, jax.random.fold_in(rng, 3), *heavy), -limit, limit).astype(kind)


def setup_inputs(seed: int = 0) -> dict:
    keys = jax.random.split(jax.random.key(seed), 3)
    return {
        "tiles": noise_with(keys[0], (2, W, N), N ** -0.5, 0.0234375, ((0, 2), (2, 16)), (2, 1, 16, 2.0), jnp.float32),
        "trial": centred(keys[1], (2, N, K), 1.0, 6.0, ((0, 2), (1, 16)), jnp.float32),
    }


def reference(tiles, trial):
    sum_vectors = trial[0] + trial[1]
    diff_vectors = trial[0] - trial[1]
    plus_products = jnp.dot(tiles[0], sum_vectors, precision=lax.Precision.HIGHEST, preferred_element_type=jnp.float32)
    minus_products = jnp.dot(tiles[1], diff_vectors, precision=lax.Precision.HIGHEST, preferred_element_type=jnp.float32)
    upper_half = 0.5 * (plus_products + minus_products)
    lower_half = 0.5 * (plus_products - minus_products)
    return jnp.stack([upper_half, lower_half])
```

```python
import functools
import math

import jax
import jax.numpy as jnp
from jax import lax
from jax.experimental import pallas as pl
from jax.experimental.pallas import tpu as pltpu
from jax.sharding import PartitionSpec as P

LANES = 128
VMEM_BYTES = 60 * 2**20


AXES = ("pair", "blk", "rows")


def swapped(value, mask):
    devices = math.prod(lax.axis_size(axis) for axis in AXES)
    return lax.ppermute(value, AXES, [(source, source ^ mask) for source in range(devices)])


def after(value, *others):
    return lax.optimization_barrier((value, *others))[0]


def parted(value, low, bits):
    mine = (lax.axis_index(AXES) >> low) & (2**bits - 1)
    value = value.reshape(-1, 2**bits, *value.shape[-2:])
    return [lax.dynamic_index_in_dim(value, mine ^ m, 1, keepdims=False) for m in range(2**bits)]


def scattered_sum(value, low, steps):
    for bits in steps:
        blocks = parted(value, low, bits)
        value = sum((swapped(blocks[m], m << low) for m in range(1, 2**bits)), blocks[0])
        low += bits
    return value


def scattered_halves(value, low, bits, sign):
    pair = 2 ** (low + bits)
    blocks = parted(value, low, bits)
    own = sum((swapped(blocks[m], m << low) for m in range(1, 2**bits)), blocks[0])
    other = sum(swapped(blocks[m], m << low | pair) for m in range(2**bits))
    return 0.5 * (other + sign * own)


def halves(value):
    high = value.astype(jnp.bfloat16)
    low = (value - high.astype(jnp.float32)).astype(jnp.bfloat16)
    return high, low


def split_kernel(matrix_ref, high_ref, low_ref):
    high_ref[...], low_ref[...] = halves(matrix_ref[...])


def split_matrix(matrix):
    rows, depth = matrix.shape
    step = min(rows, 128)
    spec = pl.BlockSpec((step, depth), lambda i: (i, 0))
    part = jax.ShapeDtypeStruct(matrix.shape, jnp.bfloat16)
    return pl.pallas_call(
        split_kernel,
        grid=(rows // step,),
        in_specs=[spec],
        out_specs=[spec, spec],
        out_shape=[part, part],
        compiler_params=pltpu.CompilerParams(vmem_limit_bytes=VMEM_BYTES),
        cost_estimate=pl.CostEstimate(flops=0, bytes_accessed=8 * rows * depth, transcendentals=0),
        name="split_matrix",
    )(matrix)


def product_kernel(added, sign_ref, *refs):
    high_ref, low_ref, own_ref, partner_ref = refs[:4]
    total_ref, out_ref, both = (refs[4:] if added else (None, *refs[4:]))
    width = out_ref.shape[1]

    @pl.when(pl.program_id(0) == 0)
    def _():
        combined = partner_ref[...] + sign_ref[0] * own_ref[...]
        both[:, :width], both[:, width:] = halves(combined)

    right = both[...]
    result = jnp.dot(low_ref[...], right, preferred_element_type=jnp.float32)
    result += jnp.dot(high_ref[...], right, preferred_element_type=jnp.float32)
    result = result[:, width:] + result[:, :width]
    out_ref[...] = result + total_ref[...] if added else result


def product(sign, high, low, own, partner, column, start, total=None):
    rows = high.shape[0]
    depth, width = partner.shape
    step = min(rows, 1024, max(256, 2**21 // depth))
    place = start // depth
    matrix_spec = pl.BlockSpec((step, depth), lambda i: (i, place))
    out_spec = pl.BlockSpec((step, width), lambda i: (i, 0))
    in_specs = [
        pl.BlockSpec(memory_space=pltpu.SMEM),
        matrix_spec,
        matrix_spec,
        pl.BlockSpec((depth, width), lambda i: (place, column)),
        pl.BlockSpec((depth, width), lambda i: (0, 0)),
    ]
    operands = [sign, high, low, own, partner]
    if total is not None:
        in_specs.append(out_spec)
        operands.append(total)
    return pl.pallas_call(
        functools.partial(product_kernel, total is not None),
        grid=(rows // step,),
        in_specs=in_specs,
        out_specs=out_spec,
        out_shape=jax.ShapeDtypeStruct((rows, width), jnp.float32),
        scratch_shapes=[pltpu.VMEM((depth, 2 * width), jnp.bfloat16)],
        compiler_params=pltpu.CompilerParams(vmem_limit_bytes=VMEM_BYTES),
        cost_estimate=pl.CostEstimate(flops=0, bytes_accessed=0, transcendentals=0),
        name="product",
    )(*operands)


def pieces_of(depth, vectors):
    last = vectors // LANES - 1
    least = max(LANES, depth // 8)
    pieces = [(last, 0, least)] + [(chunk, 0, depth) for chunk in range(last - 1)]
    pieces += [(last - 1, 0, depth // 2), (last - 1, depth // 2, depth // 2)]
    pieces += [(last, least, least), (last, depth // 2, depth // 2), (last, 2 * least, least)]
    half = max(LANES, least // 2)
    return pieces + [(last, start, half) for start in range(3 * least, depth // 2, half)]


def shards(tiles, trial):
    own, matrix = trial[0], tiles[0]
    depth, vectors = own.shape
    sign = 1.0 - 2.0 * lax.axis_index("pair").astype(jnp.float32)
    pieces = pieces_of(depth, vectors)
    pair = lax.axis_size("blk") * lax.axis_size("rows")
    bits = pair.bit_length() - 1

    def by_owner(value):
        return value.reshape(pair, -1, value.shape[-1])

    def block(index, *others):
        chunk, start, size = pieces[index]
        source = after(own, *others) if others else own
        return source[start : start + size, chunk * LANES : (chunk + 1) * LANES]

    ahead, cut_ahead = 2, 6
    blocks = {index: block(index) for index in range(ahead)}
    arrived = [swapped(blocks[index], pair) for index in range(ahead)]
    high, low = split_matrix(after(matrix, *blocks.values()))
    totals, covered, sums = {}, {}, {}
    done = high
    for index, (chunk, start, size) in enumerate(pieces):
        partner = arrived[index]
        for later in range(ahead, min(index + cut_ahead + 1, len(pieces))):
            if later not in blocks:
                blocks[later] = block(later, done)
                partner = after(partner, blocks[later])
        if index + ahead < len(pieces):
            arrived.append(swapped(after(blocks[index + ahead], arrived[index], done), pair))
        done = product(sign[None], high, low, own, partner, chunk, start, totals.get(chunk))
        totals[chunk] = done
        covered[chunk] = covered.get(chunk, 0) + size
        if covered[chunk] == depth and index + 1 < len(pieces):
            if pieces[index + 1][0] == pieces[-1][0]:
                done = after(done, arrived[index + 1])
            steps = [2] * (bits // 2) + [1] * (bits % 2)
            done = sums[chunk] = scattered_sum(by_owner(done), 0, steps)[0]

    early = jnp.concatenate([sums[chunk] for chunk in sorted(sums)], axis=1)
    early_partner = swapped(after(early, arrived[-1]), pair)
    steps = [1] + [2] * ((bits - 2) // 2) + [1] * (bits % 2)
    late = after(scattered_sum(by_owner(done), 0, steps), early_partner)
    result = jnp.concatenate(
        [0.5 * (early_partner + sign * early), scattered_halves(late, bits - 1, 1, sign)[0]], axis=1
    )
    return result[None]


def solution(mesh):
    in_specs = (P("pair", None, ("blk", "rows")), P("pair", ("blk", "rows"), None))
    out_specs = P("pair", ("blk", "rows"), None)
    return jax.shard_map(shards, mesh=mesh, in_specs=in_specs, out_specs=out_specs, check_vma=False)
```

```python
import functools
import math

import jax
import jax.numpy as jnp
from jax import lax
from jax.experimental import pallas as pl
from jax.experimental.pallas import tpu as pltpu
from jax.sharding import PartitionSpec as P

LANES = 128
VMEM_BYTES = 60 * 2**20


AXES = ("pair", "blk", "rows")


def swapped(value, mask):
    devices = math.prod(lax.axis_size(axis) for axis in AXES)
    return lax.ppermute(value, AXES, [(source, source ^ mask) for source in range(devices)])


def after(value, *others):
    return lax.optimization_barrier((value, *others))[0]


def parted(value, low, bits):
    mine = (lax.axis_index(AXES) >> low) & (2**bits - 1)
    value = value.reshape(-1, 2**bits, *value.shape[-2:])
    return [lax.dynamic_index_in_dim(value, mine ^ m, 1, keepdims=False) for m in range(2**bits)]


def scattered_sum(value, low, steps):
    for bits in steps:
        blocks = parted(value, low, bits)
        value = sum((swapped(blocks[m], m << low) for m in range(1, 2**bits)), blocks[0])
        low += bits
    return value


def scattered_halves(value, low, bits, sign):
    pair = 2 ** (low + bits)
    blocks = parted(value, low, bits)
    own = sum((swapped(blocks[m], m << low) for m in range(1, 2**bits)), blocks[0])
    other = sum(swapped(blocks[m], m << low | pair) for m in range(2**bits))
    return 0.5 * (other + sign * own)


def halves(value):
    high = value.astype(jnp.bfloat16)
    low = (value - high.astype(jnp.float32)).astype(jnp.bfloat16)
    return high, low


def split_kernel(matrix_ref, high_ref, low_ref):
    high_ref[...], low_ref[...] = halves(matrix_ref[...])


def split_matrix(matrix):
    rows, depth = matrix.shape
    step = min(rows, 128)
    spec = pl.BlockSpec((step, depth), lambda i: (i, 0))
    part = jax.ShapeDtypeStruct(matrix.shape, jnp.bfloat16)
    return pl.pallas_call(
        split_kernel,
        grid=(rows // step,),
        in_specs=[spec],
        out_specs=[spec, spec],
        out_shape=[part, part],
        compiler_params=pltpu.CompilerParams(vmem_limit_bytes=VMEM_BYTES),
        cost_estimate=pl.CostEstimate(flops=0, bytes_accessed=8 * rows * depth, transcendentals=0),
        name="split_matrix",
    )(matrix)


def product_kernel(added, sign_ref, *refs):
    high_ref, low_ref, own_ref, partner_ref = refs[:4]
    total_ref, out_ref, both = (refs[4:] if added else (None, *refs[4:]))
    width = out_ref.shape[1]

    @pl.when(pl.program_id(0) == 0)
    def _():
        combined = partner_ref[...] + sign_ref[0] * own_ref[...]
        both[:, :width], both[:, width:] = halves(combined)

    right = both[...]
    result = jnp.dot(low_ref[...], right, preferred_element_type=jnp.float32)
    result += jnp.dot(high_ref[...], right, preferred_element_type=jnp.float32)
    result = result[:, width:] + result[:, :width]
    out_ref[...] = result + total_ref[...] if added else result


def product(sign, high, low, own, partner, column, start, total=None):
    rows = high.shape[0]
    depth, width = partner.shape
    step = min(rows, 1024, max(256, 2**21 // depth))
    place = start // depth
    matrix_spec = pl.BlockSpec((step, depth), lambda i: (i, place))
    out_spec = pl.BlockSpec((step, width), lambda i: (i, 0))
    in_specs = [
        pl.BlockSpec(memory_space=pltpu.SMEM),
        matrix_spec,
        matrix_spec,
        pl.BlockSpec((depth, width), lambda i: (place, column)),
        pl.BlockSpec((depth, width), lambda i: (0, 0)),
    ]
    operands = [sign, high, low, own, partner]
    if total is not None:
        in_specs.append(out_spec)
        operands.append(total)
    return pl.pallas_call(
        functools.partial(product_kernel, total is not None),
        grid=(rows // step,),
        in_specs=in_specs,
        out_specs=out_spec,
        out_shape=jax.ShapeDtypeStruct((rows, width), jnp.float32),
        scratch_shapes=[pltpu.VMEM((depth, 2 * width), jnp.bfloat16)],
        input_output_aliases={} if total is None else {5: 0},
        compiler_params=pltpu.CompilerParams(vmem_limit_bytes=VMEM_BYTES),
        cost_estimate=pl.CostEstimate(flops=0, bytes_accessed=0, transcendentals=0),
        name="product",
    )(*operands)


def pieces_of(depth, vectors):
    last = vectors // LANES - 1
    least = max(LANES, depth // 16)
    pieces = [(last, 0, least)] + [(chunk, 0, depth) for chunk in range(last - 1)]
    pieces += [(last - 1, 0, depth // 2), (last - 1, depth // 2, depth // 2)]
    size = depth // 2
    while size >= least:
        pieces.append((last, size, size))
        size //= 2
    return pieces


def shards(tiles, trial):
    own, matrix = trial[0], tiles[0]
    depth, vectors = own.shape
    sign = 1.0 - 2.0 * lax.axis_index("pair").astype(jnp.float32)
    pieces = pieces_of(depth, vectors)
    pair = lax.axis_size("blk") * lax.axis_size("rows")
    bits = pair.bit_length() - 1

    def by_owner(value):
        return value.reshape(pair, -1, value.shape[-1])

    def block(index, *others):
        chunk, start, size = pieces[index]
        source = after(own, *others) if others else own
        return source[start : start + size, chunk * LANES : (chunk + 1) * LANES]

    ahead, cut_ahead = 2, 6
    blocks = {index: block(index) for index in range(ahead)}
    arrived = [swapped(blocks[index], pair) for index in range(ahead)]
    high, low = split_matrix(after(matrix, *blocks.values()))
    totals, covered, waiting, sums = {}, {}, [], []
    done = high
    for index, (chunk, start, size) in enumerate(pieces):
        partner = arrived[index]
        for later in range(ahead, min(index + cut_ahead + 1, len(pieces))):
            if later not in blocks:
                blocks[later] = block(later, done)
                partner = after(partner, blocks[later])
        if index + ahead < len(pieces):
            arrived.append(swapped(after(blocks[index + ahead], arrived[index], done), pair))
        done = product(sign[None], high, low, own, partner, chunk, start, totals.get(chunk))
        totals[chunk] = done
        covered[chunk] = covered.get(chunk, 0) + size
        if covered[chunk] == depth and index + 1 < len(pieces):
            waiting.append(by_owner(done))
            if len(waiting) == 2 or chunk == pieces[-1][0] - 1:
                steps = [2] * (bits // 2) + [1] * (bits % 2)
                done = scattered_sum(jnp.concatenate(waiting, axis=-1), 0, steps)[0]
                sums.append(done)
                waiting = []

    early = jnp.concatenate(sums, axis=1)
    early_partner = swapped(after(early, arrived[-1]), pair)
    steps = [1] + [2] * ((bits - 2) // 2) + [1] * (bits % 2)
    late = after(scattered_sum(by_owner(done), 0, steps), early_partner)
    result = jnp.concatenate(
        [0.5 * (early_partner + sign * early), scattered_halves(late, bits - 1, 1, sign)[0]], axis=1
    )
    return result[None]


def solution(mesh):
    in_specs = (P("pair", None, ("blk", "rows")), P("pair", ("blk", "rows"), None))
    out_specs = P("pair", ("blk", "rows"), None)
    return jax.shard_map(shards, mesh=mesh, in_specs=in_specs, out_specs=out_specs, check_vma=False)
```

```python
import functools
import math

import jax
import jax.numpy as jnp
from jax import lax
from jax.experimental import pallas as pl
from jax.experimental.pallas import tpu as pltpu
from jax.sharding import PartitionSpec as P

LANES = 128
SPLIT_BYTES = 40 * 2**20
PRODUCT_BYTES = 40 * 2**20


AXES = ("pair", "blk", "rows")


def swapped(value, mask):
    devices = math.prod(lax.axis_size(axis) for axis in AXES)
    return lax.ppermute(value, AXES, [(source, source ^ mask) for source in range(devices)])


def after(value, *others):
    return lax.optimization_barrier((value, *others))[0]


def parted(value, low, bits):
    mine = (lax.axis_index(AXES) >> low) & (2**bits - 1)
    value = value.reshape(-1, 2**bits, *value.shape[-2:])
    return [lax.dynamic_index_in_dim(value, mine ^ m, 1, keepdims=False) for m in range(2**bits)]


def scattered_sum(value, low, steps):
    for bits in steps:
        blocks = parted(value, low, bits)
        value = sum((swapped(blocks[m], m << low) for m in range(1, 2**bits)), blocks[0])
        low += bits
    return value


def scattered_halves(value, low, bits, sign):
    pair = 2 ** (low + bits)
    blocks = parted(value, low, bits)
    own = sum((swapped(blocks[m], m << low) for m in range(1, 2**bits)), blocks[0])
    other = sum(swapped(blocks[m], m << low | pair) for m in range(2**bits))
    return 0.5 * (other + sign * own)


def halves(value):
    high = value.astype(jnp.bfloat16)
    low = (value - high.astype(jnp.float32)).astype(jnp.bfloat16)
    return high, low


def split_kernel(matrix_ref, high_ref, low_ref):
    high_ref[...], low_ref[...] = halves(matrix_ref[...])


def split_matrix(matrix):
    rows, depth = matrix.shape
    step = min(rows, 128)
    spec = pl.BlockSpec((step, depth), lambda i: (i, 0))
    part = jax.ShapeDtypeStruct(matrix.shape, jnp.bfloat16)
    return pl.pallas_call(
        split_kernel,
        grid=(rows // step,),
        in_specs=[spec],
        out_specs=[spec, spec],
        out_shape=[part, part],
        compiler_params=pltpu.CompilerParams(vmem_limit_bytes=SPLIT_BYTES),
        cost_estimate=pl.CostEstimate(flops=0, bytes_accessed=8 * rows * depth, transcendentals=0),
        name="split_matrix",
    )(matrix)


def product_kernel(added, owned, control_ref, high_ref, low_ref, own_ref, partner_ref, *refs):
    total_ref = refs[0] if added else None
    out_refs, sum_ref = refs[added:-1], refs[-1]
    width = sum_ref.shape[1]
    step = pl.program_id(0)

    right = jnp.concatenate(halves(partner_ref[...] + control_ref[0] * own_ref[...]), axis=1)
    result = jnp.dot(low_ref[...], right, preferred_element_type=jnp.float32)
    result += jnp.dot(high_ref[...], right, preferred_element_type=jnp.float32)
    result = result[:, width:] + result[:, :width]

    @pl.when(step == 0)
    def _():
        sum_ref[...] = result + total_ref[...] if added else result

    @pl.when(step > 0)
    def _():
        sum_ref[...] += result

    @pl.when(step == pl.num_programs(0) - 1)
    def _():
        if owned:
            kept_ref, given_ref = out_refs
            both = sum_ref[...].reshape(-1, 2, *kept_ref.shape[1:])
            odd = control_ref[1] > 0.5
            kept_ref[...] = jnp.where(odd, both[:, 1], both[:, 0])
            given_ref[...] = jnp.where(odd, both[:, 0], both[:, 1])
        else:
            out_refs[0][...] = sum_ref[...]


def product(control, high, low, own, partner, piece, total=None, owned=0):
    chunk, start, size = piece
    rows, width = high.shape[0], partner.shape[1]
    step = 1024
    while start % step or size % step or step > max(LANES, size // 2):
        step //= 2
    first = start // step
    matrix_spec = pl.BlockSpec((rows, step), lambda i: (0, first + i))
    whole_spec = pl.BlockSpec((rows, width), lambda i: (0, 0))
    in_specs = [
        pl.BlockSpec(memory_space=pltpu.SMEM),
        matrix_spec,
        matrix_spec,
        pl.BlockSpec((step, width), lambda i: (first + i, chunk)),
        pl.BlockSpec((step, width), lambda i: (i, 0)),
    ]
    operands = [control, high, low, own, partner]
    if total is not None:
        in_specs.append(whole_spec)
        operands.append(total)
    out_specs = whole_spec
    out_shape = jax.ShapeDtypeStruct((rows, width), jnp.float32)
    if owned:
        shape = (rows // (2 * owned), owned, width)
        out_specs = [pl.BlockSpec(shape, lambda i: (0, 0, 0))] * 2
        out_shape = [jax.ShapeDtypeStruct(shape, jnp.float32)] * 2
    return pl.pallas_call(
        functools.partial(product_kernel, total is not None, owned > 0),
        grid=(size // step,),
        in_specs=in_specs,
        out_specs=out_specs,
        out_shape=out_shape,
        scratch_shapes=[pltpu.VMEM((rows, width), jnp.float32)],
        compiler_params=pltpu.CompilerParams(vmem_limit_bytes=PRODUCT_BYTES),
        cost_estimate=pl.CostEstimate(flops=0, bytes_accessed=0, transcendentals=0),
        name="product",
    )(*operands)


def pieces_of(depth, vectors):
    last = vectors // LANES - 1
    least = max(LANES, depth // 16)
    head = max(LANES, depth // 8)
    pieces = [(last, 0, head)] + [(chunk, 0, depth) for chunk in range(last - 1)]
    pieces += [(last - 1, 0, depth // 2), (last - 1, depth // 2, depth // 2)]
    start, size = head, depth // 2 - head
    while start < depth - least:
        pieces.append((last, start, size))
        start += size
        size = max(least, (depth - start) // 2)
    return pieces + [(last, start, least)]


def shards(tiles, trial):
    own, matrix = trial[0], tiles[0]
    depth, vectors = own.shape
    sign = 1.0 - 2.0 * lax.axis_index("pair").astype(jnp.float32)
    pieces = pieces_of(depth, vectors)
    odd = (lax.axis_index("rows") % 2).astype(jnp.float32)
    control = jnp.stack([sign, odd])
    pair = lax.axis_size("blk") * lax.axis_size("rows")
    bits = pair.bit_length() - 1

    def by_owner(value):
        return value.reshape(pair, -1, value.shape[-1])

    def block(index, *others):
        chunk, start, size = pieces[index]
        source = after(own, *others) if others else own
        return source[start : start + size, chunk * LANES : (chunk + 1) * LANES]

    ahead, cut_ahead = 2, 6
    blocks, arrived = {}, []
    for index in range(ahead):
        blocks[index] = block(index, *blocks.values())
        arrived.append(swapped(blocks[index], pair))
    high, low = split_matrix(after(matrix, *blocks.values()))
    totals, covered, waiting, sums = {}, {}, [], []
    done = high
    for index, (chunk, start, size) in enumerate(pieces):
        partner = arrived[index]
        for later in range(ahead, min(index + cut_ahead + 1, len(pieces))):
            if later not in blocks:
                blocks[later] = block(later, done)
                partner = after(partner, blocks[later])
        if index + ahead < len(pieces):
            arrived.append(swapped(after(blocks[index + ahead], arrived[index], done), pair))
        operands = (control, high, low, own, partner, pieces[index], totals.get(chunk))
        if index + 1 == len(pieces):
            kept, given = product(*operands, owned=matrix.shape[0] // pair)
            break
        done = totals[chunk] = product(*operands)
        covered[chunk] = covered.get(chunk, 0) + size
        if covered[chunk] == depth:
            waiting.append(by_owner(done))
            if len(waiting) == 2 or chunk == pieces[-1][0] - 1:
                steps = [2] * (bits // 2) + [1] * (bits % 2)
                done = scattered_sum(jnp.concatenate(waiting, axis=-1), 0, steps)[0]
                sums.append(done)
                waiting = []

    early = jnp.concatenate(sums, axis=1)
    early_partner = swapped(after(early, arrived[-1]), pair)
    late = kept + swapped(given, 1)
    late = scattered_sum(late, 1, [2] * ((bits - 2) // 2) + [1] * (bits % 2))
    late = after(late, early_partner)
    result = jnp.concatenate(
        [0.5 * (early_partner + sign * early), scattered_halves(late, bits - 1, 1, sign)[0]], axis=1
    )
    return result[None]


def solution(mesh):
    in_specs = (P("pair", None, ("blk", "rows")), P("pair", ("blk", "rows"), None))
    out_specs = P("pair", ("blk", "rows"), None)
    return jax.shard_map(shards, mesh=mesh, in_specs=in_specs, out_specs=out_specs, check_vma=False)
```

```python
import functools
import math

import jax
import jax.numpy as jnp
from jax import lax
from jax.experimental import pallas as pl
from jax.experimental.pallas import tpu as pltpu
from jax.sharding import PartitionSpec as P

LANES = 128
SPLIT_BYTES = 40 * 2**20
PRODUCT_BYTES = 40 * 2**20


AXES = ("pair", "blk", "rows")


def swapped(value, mask):
    devices = math.prod(lax.axis_size(axis) for axis in AXES)
    return lax.ppermute(value, AXES, [(source, source ^ mask) for source in range(devices)])


def after(value, *others):
    return lax.optimization_barrier((value, *others))[0]


def parted(value, low, bits):
    mine = (lax.axis_index(AXES) >> low) & (2**bits - 1)
    value = value.reshape(-1, 2**bits, *value.shape[-2:])
    return [lax.dynamic_index_in_dim(value, mine ^ m, 1, keepdims=False) for m in range(2**bits)]


def scattered_sum(value, low, steps):
    for bits in steps:
        blocks = parted(value, low, bits)
        value = sum((swapped(blocks[m], m << low) for m in range(1, 2**bits)), blocks[0])
        low += bits
    return value


def scattered_halves(value, low, bits, sign):
    pair = 2 ** (low + bits)
    blocks = parted(value, low, bits)
    own = sum((swapped(blocks[m], m << low) for m in range(1, 2**bits)), blocks[0])
    other = sum(swapped(blocks[m], m << low | pair) for m in range(2**bits))
    return 0.5 * (other + sign * own)


def halves(value):
    high = value.astype(jnp.bfloat16)
    low = (value - high.astype(jnp.float32)).astype(jnp.bfloat16)
    return high, low


def split_kernel(matrix_ref, high_ref, low_ref):
    high_ref[...], low_ref[...] = halves(matrix_ref[...])


def split_matrix(matrix):
    rows, depth = matrix.shape
    step = min(rows, 128)
    spec = pl.BlockSpec((step, depth), lambda i: (i, 0))
    part = jax.ShapeDtypeStruct(matrix.shape, jnp.bfloat16)
    return pl.pallas_call(
        split_kernel,
        grid=(rows // step,),
        in_specs=[spec],
        out_specs=[spec, spec],
        out_shape=[part, part],
        compiler_params=pltpu.CompilerParams(vmem_limit_bytes=SPLIT_BYTES),
        cost_estimate=pl.CostEstimate(flops=0, bytes_accessed=8 * rows * depth, transcendentals=0),
        name="split_matrix",
    )(matrix)


def product_kernel(added, owned, control_ref, high_ref, low_ref, own_ref, partner_ref, *refs):
    total_ref = refs[0] if added else None
    out_refs, sum_ref = refs[added:-1], refs[-1]
    width = sum_ref.shape[1]
    step = pl.program_id(0)

    right = jnp.concatenate(halves(partner_ref[...] + control_ref[0] * own_ref[...]), axis=1)
    result = jnp.dot(low_ref[...], right, preferred_element_type=jnp.float32)
    result += jnp.dot(high_ref[...], right, preferred_element_type=jnp.float32)
    result = result[:, width:] + result[:, :width]

    @pl.when(step == 0)
    def _():
        sum_ref[...] = result + total_ref[...] if added else result

    @pl.when(step > 0)
    def _():
        sum_ref[...] += result

    @pl.when(step == pl.num_programs(0) - 1)
    def _():
        if owned:
            kept_ref, given_ref = out_refs
            both = sum_ref[...].reshape(-1, 2, *kept_ref.shape[1:])
            odd = control_ref[1] > 0.5
            kept_ref[...] = jnp.where(odd, both[:, 1], both[:, 0])
            given_ref[...] = jnp.where(odd, both[:, 0], both[:, 1])
        else:
            out_refs[0][...] = sum_ref[...]


def product(control, high, low, own, partner, piece, total=None, owned=0):
    chunk, start, size = piece
    rows, width = high.shape[0], partner.shape[1]
    step = 1024
    while start % step or size % step or step > max(LANES, size // 2):
        step //= 2
    first = start // step
    matrix_spec = pl.BlockSpec((rows, step), lambda i: (0, first + i))
    whole_spec = pl.BlockSpec((rows, width), lambda i: (0, 0))
    in_specs = [
        pl.BlockSpec(memory_space=pltpu.SMEM),
        matrix_spec,
        matrix_spec,
        pl.BlockSpec((step, width), lambda i: (first + i, chunk)),
        pl.BlockSpec((step, width), lambda i: (i, 0)),
    ]
    operands = [control, high, low, own, partner]
    if total is not None:
        in_specs.append(whole_spec)
        operands.append(total)
    out_specs = whole_spec
    out_shape = jax.ShapeDtypeStruct((rows, width), jnp.float32)
    if owned:
        shape = (rows // (2 * owned), owned, width)
        out_specs = [pl.BlockSpec(shape, lambda i: (0, 0, 0))] * 2
        out_shape = [jax.ShapeDtypeStruct(shape, jnp.float32)] * 2
    return pl.pallas_call(
        functools.partial(product_kernel, total is not None, owned > 0),
        grid=(size // step,),
        in_specs=in_specs,
        out_specs=out_specs,
        out_shape=out_shape,
        scratch_shapes=[pltpu.VMEM((rows, width), jnp.float32)],
        compiler_params=pltpu.CompilerParams(vmem_limit_bytes=PRODUCT_BYTES),
        cost_estimate=pl.CostEstimate(flops=0, bytes_accessed=0, transcendentals=0),
        name="product",
    )(*operands)


def pieces_of(depth, vectors):
    last = vectors // LANES - 1
    least = max(LANES, depth // 16)
    head = max(LANES, depth // 8)
    pieces = [(last, 0, head)] + [(chunk, 0, depth) for chunk in range(last - 1)]
    pieces += [(last - 1, 0, depth // 2), (last - 1, depth // 2, depth // 2)]
    start, size = head, depth // 2 - head
    while start < depth - least:
        pieces.append((last, start, size))
        start += size
        size = max(least, (depth - start) // 2)
    return pieces + [(last, start, least)]


def shards(tiles, trial):
    own, matrix = trial[0], tiles[0]
    depth, vectors = own.shape
    sign = 1.0 - 2.0 * lax.axis_index("pair").astype(jnp.float32)
    pieces = pieces_of(depth, vectors)
    odd = (lax.axis_index("rows") % 2).astype(jnp.float32)
    control = jnp.stack([sign, odd])
    pair = lax.axis_size("blk") * lax.axis_size("rows")
    bits = pair.bit_length() - 1

    def by_owner(value):
        return value.reshape(pair, -1, value.shape[-1])

    def block(index, *others):
        chunk, start, size = pieces[index]
        source = after(own, *others) if others else own
        return source[start : start + size, chunk * LANES : (chunk + 1) * LANES]

    ahead, cut_ahead = 2, 6
    blocks, arrived = {}, []
    for index in range(ahead):
        blocks[index] = block(index, *blocks.values())
        arrived.append(swapped(blocks[index], pair))
    high, low = split_matrix(after(matrix, *blocks.values()))
    totals, covered, waiting, sums = {}, {}, [], []
    done = high
    for index, (chunk, start, size) in enumerate(pieces):
        partner = arrived[index]
        for later in range(ahead, min(index + cut_ahead + 1, len(pieces))):
            if later not in blocks:
                blocks[later] = block(later, done)
                partner = after(partner, blocks[later])
        ready = index + ahead + (index + ahead >= len(pieces) - 4)
        while len(arrived) < min(ready + 1, len(pieces)):
            arrived.append(swapped(after(blocks[len(arrived)], arrived[index], done), pair))
        operands = (control, high, low, own, partner, pieces[index], totals.get(chunk))
        if index + 1 == len(pieces):
            kept, given = product(*operands, owned=matrix.shape[0] // pair)
            break
        done = totals[chunk] = product(*operands)
        covered[chunk] = covered.get(chunk, 0) + size
        if covered[chunk] == depth:
            waiting.append(by_owner(done))
            if len(waiting) == 2 or chunk == pieces[-1][0] - 1:
                steps = [2] * (bits // 2) + [1] * (bits % 2)
                done = scattered_sum(jnp.concatenate(waiting, axis=-1), 0, steps)[0]
                sums.append(done)
                waiting = []

    early = jnp.concatenate(sums, axis=1)
    early_partner = swapped(after(early, arrived[-1]), pair)
    late = kept + swapped(given, 1)
    late = scattered_sum(late, 1, [2] * ((bits - 2) // 2) + [1] * (bits % 2))
    late = after(late, early_partner)
    result = jnp.concatenate(
        [0.5 * (early_partner + sign * early), scattered_halves(late, bits - 1, 1, sign)[0]], axis=1
    )
    return result[None]


def solution(mesh):
    in_specs = (P("pair", None, ("blk", "rows")), P("pair", ("blk", "rows"), None))
    out_specs = P("pair", ("blk", "rows"), None)
    return jax.shard_map(shards, mesh=mesh, in_specs=in_specs, out_specs=out_specs, check_vma=False)
```

```python
import functools
import math

import jax
import jax.numpy as jnp
from jax import lax
from jax.experimental import pallas as pl
from jax.experimental.pallas import tpu as pltpu
from jax.sharding import PartitionSpec as P

LANES = 128
SPLIT_BYTES = 40 * 2**20
PRODUCT_BYTES = 40 * 2**20


AXES = ("pair", "blk", "rows")


def swapped(value, mask):
    devices = math.prod(lax.axis_size(axis) for axis in AXES)
    return lax.ppermute(value, AXES, [(source, source ^ mask) for source in range(devices)])


def after(value, *others):
    return lax.optimization_barrier((value, *others))[0]


def parted(value, low, bits):
    mine = (lax.axis_index(AXES) >> low) & (2**bits - 1)
    value = value.reshape(-1, 2**bits, *value.shape[-2:])
    return [lax.dynamic_index_in_dim(value, mine ^ m, 1, keepdims=False) for m in range(2**bits)]


def scattered_sum(value, low, steps):
    for bits in steps:
        blocks = parted(value, low, bits)
        value = sum((swapped(blocks[m], m << low) for m in range(1, 2**bits)), blocks[0])
        low += bits
    return value


def scattered_halves(value, low, bits, sign):
    pair = 2 ** (low + bits)
    blocks = parted(value, low, bits)
    own = sum((swapped(blocks[m], m << low) for m in range(1, 2**bits)), blocks[0])
    other = sum(swapped(blocks[m], m << low | pair) for m in range(2**bits))
    return 0.5 * (other + sign * own)


def halves(value):
    high = value.astype(jnp.bfloat16)
    low = (value - high.astype(jnp.float32)).astype(jnp.bfloat16)
    return high, low


def split_kernel(matrix_ref, high_ref, low_ref):
    high_ref[...], low_ref[...] = halves(matrix_ref[...])


def split_matrix(matrix):
    rows, depth = matrix.shape
    step = min(rows, 128)
    spec = pl.BlockSpec((step, depth), lambda i: (i, 0))
    part = jax.ShapeDtypeStruct(matrix.shape, jnp.bfloat16)
    return pl.pallas_call(
        split_kernel,
        grid=(rows // step,),
        in_specs=[spec],
        out_specs=[spec, spec],
        out_shape=[part, part],
        compiler_params=pltpu.CompilerParams(vmem_limit_bytes=SPLIT_BYTES),
        cost_estimate=pl.CostEstimate(flops=0, bytes_accessed=8 * rows * depth, transcendentals=0),
        name="split_matrix",
    )(matrix)


def product_kernel(added, owned, control_ref, high_ref, low_ref, own_ref, partner_ref, *refs):
    total_ref = refs[0] if added else None
    out_refs, sum_ref = refs[added:-1], refs[-1]
    width = sum_ref.shape[1]
    step = pl.program_id(0)

    right = jnp.concatenate(halves(partner_ref[...] + control_ref[0] * own_ref[...]), axis=1)
    result = jnp.dot(low_ref[...], right, preferred_element_type=jnp.float32)
    result += jnp.dot(high_ref[...], right, preferred_element_type=jnp.float32)
    result = result[:, width:] + result[:, :width]

    @pl.when(step == 0)
    def _():
        sum_ref[...] = result + total_ref[...] if added else result

    @pl.when(step > 0)
    def _():
        sum_ref[...] += result

    @pl.when(step == pl.num_programs(0) - 1)
    def _():
        if owned:
            kept_ref, given_ref = out_refs
            both = sum_ref[...].reshape(-1, 2, *kept_ref.shape[1:])
            odd = control_ref[1] > 0.5
            kept_ref[...] = jnp.where(odd, both[:, 1], both[:, 0])
            given_ref[...] = jnp.where(odd, both[:, 0], both[:, 1])
        else:
            out_refs[0][...] = sum_ref[...]


def product(control, high, low, own, partner, piece, total=None, owned=0):
    chunk, start, size = piece
    rows, width = high.shape[0], partner.shape[1]
    step = 1024
    while start % step or size % step or step > max(LANES, size // 2):
        step //= 2
    first = start // step
    matrix_spec = pl.BlockSpec((rows, step), lambda i: (0, first + i))
    whole_spec = pl.BlockSpec((rows, width), lambda i: (0, 0))
    in_specs = [
        pl.BlockSpec(memory_space=pltpu.SMEM),
        matrix_spec,
        matrix_spec,
        pl.BlockSpec((step, width), lambda i: (first + i, chunk)),
        pl.BlockSpec((step, width), lambda i: (i, 0)),
    ]
    operands = [control, high, low, own, partner]
    if total is not None:
        in_specs.append(whole_spec)
        operands.append(total)
    out_specs = whole_spec
    out_shape = jax.ShapeDtypeStruct((rows, width), jnp.float32)
    if owned:
        shape = (rows // (2 * owned), owned, width)
        out_specs = [pl.BlockSpec(shape, lambda i: (0, 0, 0))] * 2
        out_shape = [jax.ShapeDtypeStruct(shape, jnp.float32)] * 2
    return pl.pallas_call(
        functools.partial(product_kernel, total is not None, owned > 0),
        grid=(size // step,),
        in_specs=in_specs,
        out_specs=out_specs,
        out_shape=out_shape,
        scratch_shapes=[pltpu.VMEM((rows, width), jnp.float32)],
        compiler_params=pltpu.CompilerParams(vmem_limit_bytes=PRODUCT_BYTES),
        cost_estimate=pl.CostEstimate(flops=0, bytes_accessed=0, transcendentals=0),
        name="product",
    )(*operands)


def pieces_of(depth, vectors):
    last = vectors // LANES - 1
    least = max(LANES, depth // 16)
    head = max(LANES, depth // 8)
    pieces = [(last, 0, head)] + [(chunk, 0, depth) for chunk in range(last - 1)]
    pieces += [(last - 1, 0, depth // 2), (last - 1, depth // 2, depth // 2)]
    start, size = head, depth // 2 - head
    while start < depth - least:
        pieces.append((last, start, size))
        start += size
        size = max(least, (depth - start) // 2)
    return pieces + [(last, start, least)]


def shards(tiles, trial):
    own, matrix = trial[0], tiles[0]
    depth, vectors = own.shape
    sign = 1.0 - 2.0 * lax.axis_index("pair").astype(jnp.float32)
    pieces = pieces_of(depth, vectors)
    odd = (lax.axis_index("rows") % 2).astype(jnp.float32)
    control = jnp.stack([sign, odd])
    pair = lax.axis_size("blk") * lax.axis_size("rows")
    bits = pair.bit_length() - 1

    def by_owner(value):
        return value.reshape(pair, -1, value.shape[-1])

    def block(index, *others):
        chunk, start, size = pieces[index]
        source = after(own, *others) if others else own
        return source[start : start + size, chunk * LANES : (chunk + 1) * LANES]

    ahead, cut_ahead = 2, 6
    blocks, arrived = {}, []
    for index in range(ahead):
        blocks[index] = block(index, *blocks.values())
        arrived.append(swapped(blocks[index], pair))
    high, low = split_matrix(after(matrix, *blocks.values()))
    totals, covered, waiting, sums = {}, {}, [], []
    done = high
    for index, (chunk, start, size) in enumerate(pieces):
        partner = arrived[index]
        for later in range(ahead, min(index + cut_ahead + 1, len(pieces))):
            if later not in blocks:
                blocks[later] = block(later, done)
                partner = after(partner, blocks[later])
        if index + ahead < len(pieces):
            arrived.append(swapped(after(blocks[index + ahead], arrived[index], done), pair))
        operands = (control, high, low, own, partner, pieces[index], totals.get(chunk))
        if index + 1 == len(pieces):
            kept, given = product(*operands, owned=matrix.shape[0] // pair)
            break
        done = totals[chunk] = product(*operands)
        covered[chunk] = covered.get(chunk, 0) + size
        if covered[chunk] == depth:
            waiting.append(by_owner(done))
            if len(waiting) == 2 or chunk == pieces[-1][0] - 1:
                steps = [2] * (bits // 2) + [1] * (bits % 2)
                done = scattered_sum(jnp.concatenate(waiting, axis=-1), 0, steps)[0]
                sums.append(done)
                waiting = []

    first, rest = sums[0], jnp.concatenate(sums[1:], axis=1)
    first_partner = swapped(after(first, arrived[-1]), pair)
    rest_partner = swapped(after(rest, first_partner), pair)
    late = kept + swapped(given, 1)
    late = scattered_sum(late, 1, [2] * ((bits - 2) // 2) + [1] * (bits % 2))
    late = after(scattered_sum(late, bits - 1, [1])[0], rest_partner)
    late_partner = swapped(late, pair)
    early = [0.5 * (first_partner + sign * first), 0.5 * (rest_partner + sign * rest)]
    result = jnp.concatenate([*early, 0.5 * (late_partner + sign * late)], axis=1)
    return result[None]


def solution(mesh):
    in_specs = (P("pair", None, ("blk", "rows")), P("pair", ("blk", "rows"), None))
    out_specs = P("pair", ("blk", "rows"), None)
    return jax.shard_map(shards, mesh=mesh, in_specs=in_specs, out_specs=out_specs, check_vma=False)
```

```python
import functools
import math

import jax
import jax.numpy as jnp
from jax import lax
from jax.experimental import pallas as pl
from jax.experimental.pallas import tpu as pltpu
from jax.sharding import PartitionSpec as P

LANES = 128
SPLIT_BYTES = 40 * 2**20
PRODUCT_BYTES = 40 * 2**20


AXES = ("pair", "blk", "rows")


def swapped(value, mask):
    devices = math.prod(lax.axis_size(axis) for axis in AXES)
    return lax.ppermute(value, AXES, [(source, source ^ mask) for source in range(devices)])


def after(value, *others):
    return lax.optimization_barrier((value, *others))[0]


def parted(value, low, bits):
    mine = (lax.axis_index(AXES) >> low) & (2**bits - 1)
    value = value.reshape(-1, 2**bits, *value.shape[-2:])
    return [lax.dynamic_index_in_dim(value, mine ^ m, 1, keepdims=False) for m in range(2**bits)]


def scattered_sum(value, low, steps):
    for bits in steps:
        blocks = parted(value, low, bits)
        value = sum((swapped(blocks[m], m << low) for m in range(1, 2**bits)), blocks[0])
        low += bits
    return value


def scattered_halves(value, low, bits, sign):
    pair = 2 ** (low + bits)
    blocks = parted(value, low, bits)
    own = sum((swapped(blocks[m], m << low) for m in range(1, 2**bits)), blocks[0])
    other = sum(swapped(blocks[m], m << low | pair) for m in range(2**bits))
    return 0.5 * (other + sign * own)


def halves(value):
    high = value.astype(jnp.bfloat16)
    low = (value - high.astype(jnp.float32)).astype(jnp.bfloat16)
    return high, low


def split_kernel(matrix_ref, high_ref, low_ref):
    high_ref[...], low_ref[...] = halves(matrix_ref[...])


def split_matrix(matrix):
    rows, depth = matrix.shape
    step = min(rows, 128)
    spec = pl.BlockSpec((step, depth), lambda i: (i, 0))
    part = jax.ShapeDtypeStruct(matrix.shape, jnp.bfloat16)
    return pl.pallas_call(
        split_kernel,
        grid=(rows // step,),
        in_specs=[spec],
        out_specs=[spec, spec],
        out_shape=[part, part],
        compiler_params=pltpu.CompilerParams(vmem_limit_bytes=SPLIT_BYTES),
        cost_estimate=pl.CostEstimate(flops=0, bytes_accessed=8 * rows * depth, transcendentals=0),
        name="split_matrix",
    )(matrix)


def product_kernel(added, owned, control_ref, high_ref, low_ref, own_ref, partner_ref, *refs):
    total_ref = refs[0] if added else None
    out_refs, sum_ref = refs[added:-1], refs[-1]
    width = sum_ref.shape[1]
    step = pl.program_id(0)

    right = jnp.concatenate(halves(partner_ref[...] + control_ref[0] * own_ref[...]), axis=1)
    result = jnp.dot(low_ref[...], right, preferred_element_type=jnp.float32)
    result += jnp.dot(high_ref[...], right, preferred_element_type=jnp.float32)
    result = result[:, width:] + result[:, :width]

    @pl.when(step == 0)
    def _():
        sum_ref[...] = result + total_ref[...] if added else result

    @pl.when(step > 0)
    def _():
        sum_ref[...] += result

    @pl.when(step == pl.num_programs(0) - 1)
    def _():
        if owned:
            kept_ref, given_ref = out_refs
            both = sum_ref[...].reshape(-1, 2, *kept_ref.shape[1:])
            odd = control_ref[1] > 0.5
            kept_ref[...] = jnp.where(odd, both[:, 1], both[:, 0])
            given_ref[...] = jnp.where(odd, both[:, 0], both[:, 1])
        else:
            out_refs[0][...] = sum_ref[...]


def product(control, high, low, own, partner, piece, total=None, owned=0):
    chunk, start, size = piece
    rows, width = high.shape[0], partner.shape[1]
    step = 1024
    while start % step or size % step or step > max(LANES, size // 2):
        step //= 2
    first = start // step
    matrix_spec = pl.BlockSpec((rows, step), lambda i: (0, first + i))
    whole_spec = pl.BlockSpec((rows, width), lambda i: (0, 0))
    in_specs = [
        pl.BlockSpec(memory_space=pltpu.SMEM),
        matrix_spec,
        matrix_spec,
        pl.BlockSpec((step, width), lambda i: (first + i, chunk)),
        pl.BlockSpec((step, width), lambda i: (i, 0)),
    ]
    operands = [control, high, low, own, partner]
    if total is not None:
        in_specs.append(whole_spec)
        operands.append(total)
    out_specs = whole_spec
    out_shape = jax.ShapeDtypeStruct((rows, width), jnp.float32)
    if owned:
        shape = (rows // (2 * owned), owned, width)
        out_specs = [pl.BlockSpec(shape, lambda i: (0, 0, 0))] * 2
        out_shape = [jax.ShapeDtypeStruct(shape, jnp.float32)] * 2
    return pl.pallas_call(
        functools.partial(product_kernel, total is not None, owned > 0),
        grid=(size // step,),
        in_specs=in_specs,
        out_specs=out_specs,
        out_shape=out_shape,
        scratch_shapes=[pltpu.VMEM((rows, width), jnp.float32)],
        compiler_params=pltpu.CompilerParams(vmem_limit_bytes=PRODUCT_BYTES),
        cost_estimate=pl.CostEstimate(flops=0, bytes_accessed=0, transcendentals=0),
        name="product",
    )(*operands)


def pieces_of(depth, vectors):
    last = vectors // LANES - 1
    least = max(LANES, depth // 16)
    head = max(LANES, depth // 8)
    pieces = [(last, 0, head)] + [(chunk, 0, depth) for chunk in range(last - 1)]
    pieces += [(last - 1, 0, depth // 2), (last - 1, depth // 2, depth // 2)]
    start, size = head, depth // 2 - head
    while start < depth - least:
        pieces.append((last, start, size))
        start += size
        size = max(least, (depth - start) // 2)
    return pieces + [(last, start, least)]


def shards(tiles, trial):
    own, matrix = trial[0], tiles[0]
    depth, vectors = own.shape
    sign = 1.0 - 2.0 * lax.axis_index("pair").astype(jnp.float32)
    pieces = pieces_of(depth, vectors)
    odd = (lax.axis_index("rows") % 2).astype(jnp.float32)
    control = jnp.stack([sign, odd])
    pair = lax.axis_size("blk") * lax.axis_size("rows")
    bits = pair.bit_length() - 1

    def by_owner(value):
        return value.reshape(pair, -1, value.shape[-1])

    def block(index, *others):
        chunk, start, size = pieces[index]
        source = after(own, *others) if others else own
        return source[start : start + size, chunk * LANES : (chunk + 1) * LANES]

    ahead, cut_ahead = 2, 6
    blocks, arrived = {}, []
    for index in range(ahead):
        blocks[index] = block(index, *blocks.values())
        arrived.append(swapped(blocks[index], pair))
    high, low = split_matrix(after(matrix, *blocks.values()))
    totals, covered, waiting, sums = {}, {}, [], []
    done = high
    for index, (chunk, start, size) in enumerate(pieces):
        partner = arrived[index]
        for later in range(ahead, min(index + cut_ahead + 1, len(pieces))):
            if later not in blocks:
                blocks[later] = block(later, done)
                partner = after(partner, blocks[later])
        ready = index + ahead + (index + ahead >= len(pieces) - 4)
        while len(arrived) < min(ready + 1, len(pieces)):
            arrived.append(swapped(after(blocks[len(arrived)], arrived[index], done), pair))
        operands = (control, high, low, own, partner, pieces[index], totals.get(chunk))
        if index + 1 == len(pieces):
            kept, given = product(*operands, owned=matrix.shape[0] // pair)
            break
        done = totals[chunk] = product(*operands)
        covered[chunk] = covered.get(chunk, 0) + size
        if covered[chunk] == depth:
            waiting.append(by_owner(done))
            if len(waiting) == 2 or chunk == pieces[-1][0] - 1:
                steps = [2] * (bits // 2) + [1] * (bits % 2)
                done = scattered_sum(jnp.concatenate(waiting, axis=-1), 0, steps)[0]
                sums.append(done)
                waiting = []

    first, rest = sums[0], jnp.concatenate(sums[1:], axis=1)
    first_partner = swapped(after(first, arrived[-1]), pair)
    rest_partner = swapped(after(rest, first_partner), pair)
    late = kept + swapped(given, 1)
    late = scattered_sum(late, 1, [2] * ((bits - 2) // 2) + [1] * (bits % 2))
    late = after(scattered_sum(late, bits - 1, [1])[0], rest_partner)
    late_partner = swapped(late, pair)
    early = [0.5 * (first_partner + sign * first), 0.5 * (rest_partner + sign * rest)]
    result = jnp.concatenate([*early, 0.5 * (late_partner + sign * late)], axis=1)
    return result[None]


def solution(mesh):
    in_specs = (P("pair", None, ("blk", "rows")), P("pair", ("blk", "rows"), None))
    out_specs = P("pair", ("blk", "rows"), None)
    return jax.shard_map(shards, mesh=mesh, in_specs=in_specs, out_specs=out_specs, check_vma=False)
```
